32 devices in a mesh: sec: 4 (over y, x), bulk: 8 (over z, core).
Axes of the slice: x: 2, y: 2, z: 4, core: 2. Of those that a mesh axis runs over, the one named last changes fastest.
Arguments:
- modes_x: bfloat16 [96, 4, 32, 8, 128], P(None, 'sec', 'bulk'), may hold values from -30 to 30
- modes_p: bfloat16 [96, 4, 32, 8, 128], P(None, 'sec', 'bulk'), may hold values from -30 to 30
- ritz_values: float32 [96], replicated, may hold values from 0.05 to 2
- node_types: int32 [4, 32, 8, 128], P('sec', 'bulk'), may hold values from 0 to 7
- stiff_table: float32 [8], replicated, may hold values from 1 to 10
- mass_table: float32 [8], replicated, may hold values from 0.5 to 4
- joint_nodes: int32 [4, 8, 4, 128], P('sec', 'bulk'), may hold values from 0 to 4095
- joint_count: int32 [4, 8, 4], P('sec', 'bulk'), may hold values from 0 to 128, as said below
Outputs:
- search_dir: bfloat16 [96, 4, 32, 8, 128], P(None, 'sec', 'bulk')
- ritz_pencil: float32 [288, 288], replicated
The draws below stay inside these ranges and needn't reach their ends.
Inputs may be any that keep to these rules, and one draw needn't show every extreme that they name: `joint_nodes`: local node numbers of a slab; slots at or beyond the count are ignored; a node may appear in several slots. Symmetric: joint_count[a, b, c] = joint_count[c, b, a], zero for a = c.
All inputs are finite; a program needn't handle non-finite values.
Results may differ from the reference program's by a relative error of at most 0.0004.
The reference program's roundings to bfloat16 on the way (of `kappa` and `span`) count: a program that leaves them out, or rounds other values in their place, can miss the bound.
Values may be sent and summed in bfloat16 or wider, within the bound.
A program may use at most 64 MiB of HBM per device.

```python
import math
import jax
import jax.numpy as jnp
from jax import lax

MODES = 96
COLS = 288
CX = 128
CY = 8
CZ = 4
FACE_CAP = 128
NTYPE = 8
SECS = 4
SLABS = 8
NZ = 32


def draw_joint_count(key, part):
    upper = jax.random.randint(jax.random.fold_in(key, 11), (SLABS, SECS, SECS), FACE_CAP // 4, FACE_CAP + 1)
    upper = jnp.triu(upper, 1)
    first = jax.random.randint(jax.random.fold_in(key, 12), (), 0, SECS - 1)
    rows = jnp.arange(SECS, dtype=jnp.int32)[:, None]
    cols = jnp.arange(SECS, dtype=jnp.int32)[None, :]
    chosen = jnp.logical_and(rows == first, cols == first + 1)
    upper = jnp.where(chosen[None], FACE_CAP, upper)
    full = upper + jnp.transpose(upper, (0, 2, 1))
    return jnp.transpose(full, (1, 0, 2)).astype(jnp.int32)


def block_amplitude(key):
    level = jax.random.uniform(jax.random.fold_in(key, 21), (SECS, SLABS), jnp.float32, math.log(0.2), math.log(5.0))
    amplitude = jnp.exp(level)
    return jnp.repeat(amplitude, CZ, axis=1)[None, :, :, None, None]


def block_values(key, salt):
    shape = (MODES, SECS, NZ, CY, CX)
    noise = jnp.clip(jax.random.normal(jax.random.fold_in(key, salt), shape, jnp.float32), -6.0, 6.0)
    return (noise * block_amplitude(key)).astype(jnp.bfloat16)


def draw_modes_x(key, part):
    return block_values(key, 22)


def draw_modes_p(key, part):
    return block_values(key, 23)


def plant(array, stream_key, smallest, largest):
    place = [jax.random.randint(jax.random.fold_in(stream_key, axis), (), 0, length) for axis, length in enumerate(array.shape)]
    widest = array.shape.index(max(array.shape))
    next_to = place[:widest] + [(place[widest] + 1) % array.shape[widest]] + place[widest + 1:]
    return array.at[tuple(place)].set(smallest).at[tuple(next_to)].set(largest)


def setup_inputs(seed: int = 0) -> dict:
    key_of = jax.random.split(jax.random.key(seed), 9)
    modes_x = draw_modes_x(jax.random.fold_in(key_of[8], 71), 0)
    modes_p = draw_modes_p(jax.random.fold_in(key_of[8], 71), 0)
    ritz_values = jnp.clip(jnp.exp(jax.random.uniform(key_of[2], (MODES,), jnp.float32, math.log(0.05), math.log(2.0))), 0.05, 2.0)
    node_types = plant(jax.random.randint(key_of[3], (SECS, NZ, CY, CX), 0, NTYPE), jax.random.fold_in(key_of[3], 1), 0, NTYPE - 1).astype(jnp.int32)
    stiff_table = jnp.clip(jnp.exp(jax.random.uniform(key_of[4], (NTYPE,), jnp.float32, math.log(1.0), math.log(10.0))), 1.0, 10.0)
    mass_table = jnp.clip(jnp.exp(jax.random.uniform(key_of[5], (NTYPE,), jnp.float32, math.log(0.5), math.log(4.0))), 0.5, 4.0)
    joint_nodes = plant(jax.random.randint(key_of[6], (SECS, SLABS, SECS, FACE_CAP), 0, CZ * CY * CX), jax.random.fold_in(key_of[6], 1), 0, (CZ * CY * CX) - 1).astype(jnp.int32)
    joint_count = draw_joint_count(jax.random.fold_in(key_of[8], 71), 0)
    return {"modes_x": modes_x, "modes_p": modes_p, "ritz_values": ritz_values, "node_types": node_types, "stiff_table": stiff_table, "mass_table": mass_table, "joint_nodes": joint_nodes, "joint_count": joint_count}


JOINT_GAIN = 0.5
SPRING = (0.0, 0.1, 0.05, 0.025)
OFFSETS = [(step_z, step_y, step_x) for step_z in (-1, 0, 1) for step_y in (-1, 0, 1) for step_x in (-1, 0, 1) if (step_z, step_y, step_x) != (0, 0, 0)]

def lower_solve(lower, matrix):
    return lax.linalg.triangular_solve(lower, matrix, left_side=True, lower=True)

def edge_weights(kappa_pad):
    padded = jnp.pad(kappa_pad.astype(jnp.float32), ((0, 0), (1, 1), (1, 1)))
    depth = padded.shape[0] - 2
    height = padded.shape[1] - 2
    breadth = padded.shape[2] - 2
    centre = padded[1:-1, 1:-1, 1:-1]
    weights = []
    summed = jnp.zeros(centre.shape, jnp.float32)
    for offset in OFFSETS:
        step_z, step_y, step_x = offset
        other = padded[1 + step_z:1 + step_z + depth, 1 + step_y:1 + step_y + height, 1 + step_x:1 + step_x + breadth]
        reach = abs(step_z) + abs(step_y) + abs(step_x)
        weight = SPRING[reach] * 2.0 * centre * other / (centre + other)
        weights.append(weight)
        summed = summed + weight
    return (weights, summed)

def apply_stencil(values_pad, weights, summed):
    padded = jnp.pad(values_pad, ((0, 0), (0, 0), (1, 1), (1, 1)))
    depth = padded.shape[1] - 2
    height = padded.shape[2] - 2
    breadth = padded.shape[3] - 2
    accum = jnp.zeros((padded.shape[0], depth, height, breadth), jnp.float32)
    for offset, weight in zip(OFFSETS, weights):
        step_z, step_y, step_x = offset
        other = padded[:, 1 + step_z:1 + step_z + depth, 1 + step_y:1 + step_y + height, 1 + step_x:1 + step_x + breadth]
        accum = accum + weight[None] * other.astype(jnp.float32)
    centre = padded[:, 1:-1, 1:-1, 1:-1].astype(jnp.float32)
    return summed[None] * centre - accum

def joint_apply(result, sent, recv, node_ids, joint_w):
    width = result.shape[0]
    delta = joint_w.reshape(1, -1) * (sent.astype(jnp.float32) - recv.astype(jnp.float32)).reshape(width, -1)
    return result.reshape(width, -1).at[:, node_ids].add(delta).reshape(result.shape)

def mirror(matrix):
    return jnp.triu(matrix) + jnp.transpose(jnp.triu(matrix, 1))

def reference(modes_x, modes_p, ritz_values, node_types, stiff_table, mass_table, joint_nodes, joint_count):
    nodes = CZ * CY * CX
    kappa = jnp.take(stiff_table, node_types).astype(jnp.bfloat16)
    mass = jnp.take(mass_table, node_types)
    node_ids = joint_nodes.reshape(SECS, SLABS, SECS * FACE_CAP)
    live = (jnp.arange(FACE_CAP, dtype=jnp.int32)[None, None, None, :] < joint_count[:, :, :, None]).astype(jnp.float32)
    shifts = (jnp.arange(SLABS, dtype=jnp.int32) * nodes)[None, :, None]
    section_ids = (node_ids + shifts).reshape(SECS, SLABS * SECS * FACE_CAP)

    def faces(block):
        width = block.shape[0]
        flat = block.reshape(width, SECS, SLABS, nodes)
        sent = jnp.take_along_axis(flat, node_ids[None], axis=3).reshape(width, SECS, SLABS, SECS, FACE_CAP)
        return (sent, jnp.transpose(sent, (0, 3, 2, 1, 4)))
    kappa_sent, kappa_recv = faces(kappa[None])
    own = kappa_sent[0].astype(jnp.float32)
    other = kappa_recv[0].astype(jnp.float32)
    joint_all = JOINT_GAIN * 2.0 * own * other / (own + other) * live
    x_sent, x_recv = faces(modes_x)

    def section_setup(index):
        kappa_sec = lax.dynamic_index_in_dim(kappa, index, 0, keepdims=False)
        weights, summed = edge_weights(jnp.pad(kappa_sec, ((1, 1), (0, 0), (0, 0))))
        joint_sec = lax.dynamic_index_in_dim(joint_all, index, 0, keepdims=False)
        ids_sec = lax.dynamic_index_in_dim(section_ids, index, 0, keepdims=False)
        return (weights, summed, joint_sec, ids_sec)

    def stiffness(block, sent, recv, index, weights, summed, joint_sec, ids_sec):
        block_sec = lax.dynamic_index_in_dim(block, index, 1, keepdims=False)
        sent_sec = lax.dynamic_index_in_dim(sent, index, 1, keepdims=False)
        recv_sec = lax.dynamic_index_in_dim(recv, index, 1, keepdims=False)
        padded = jnp.pad(block_sec, ((0, 0), (1, 1), (0, 0), (0, 0)))
        result = apply_stencil(padded, weights, summed)
        return joint_apply(result, sent_sec, recv_sec, ids_sec, joint_sec)

    def first_pass(index):
        weights, summed, joint_sec, ids_sec = section_setup(index)
        diag_full = summed.reshape(-1).at[ids_sec].add(joint_sec.reshape(-1)).reshape(summed.shape)
        stiff_x = stiffness(modes_x, x_sent, x_recv, index, weights, summed, joint_sec, ids_sec)
        x_sec = lax.dynamic_index_in_dim(modes_x, index, 1, keepdims=False)
        mass_sec = lax.dynamic_index_in_dim(mass, index, 0, keepdims=False)
        resid = stiff_x - mass_sec[None] * x_sec.astype(jnp.float32) * ritz_values[:, None, None, None]
        return (resid / diag_full[None]).astype(jnp.bfloat16)
    search_sec = lax.map(first_pass, jnp.arange(SECS, dtype=jnp.int32))
    search_dir = jnp.moveaxis(search_sec, 0, 1)
    w_sent, w_recv = faces(search_dir)
    p_sent, p_recv = faces(modes_p)

    def second_pass(carry, index):
        weights, summed, joint_sec, ids_sec = section_setup(index)
        stiff_x = stiffness(modes_x, x_sent, x_recv, index, weights, summed, joint_sec, ids_sec)
        stiff_w = stiffness(search_dir, w_sent, w_recv, index, weights, summed, joint_sec, ids_sec)
        stiff_p = stiffness(modes_p, p_sent, p_recv, index, weights, summed, joint_sec, ids_sec)
        span = jnp.concatenate([lax.dynamic_index_in_dim(modes_x, index, 1, keepdims=False), lax.dynamic_index_in_dim(search_dir, index, 1, keepdims=False), lax.dynamic_index_in_dim(modes_p, index, 1, keepdims=False)], axis=0).reshape(COLS, -1)
        stiff_span = jnp.concatenate([stiff_x, stiff_w, stiff_p], axis=0).astype(jnp.bfloat16).reshape(COLS, -1)
        mass_sec = lax.dynamic_index_in_dim(mass, index, 0, keepdims=False).reshape(1, -1)
        mass_span = (mass_sec * span.astype(jnp.float32)).astype(jnp.bfloat16)
        gram_k = carry[0] + jnp.dot(span.astype(jnp.float32), jnp.transpose(stiff_span).astype(jnp.float32), preferred_element_type=jnp.float32)
        gram_m = carry[1] + jnp.dot(span.astype(jnp.float32), jnp.transpose(mass_span).astype(jnp.float32), preferred_element_type=jnp.float32)
        return ((gram_k, gram_m), None)
    zeros = jnp.zeros((COLS, COLS), jnp.float32)
    (gram_k, gram_m), unused = lax.scan(second_pass, (zeros, zeros), jnp.arange(SECS, dtype=jnp.int32))
    stiff_gram = mirror(gram_k)
    mass_gram = mirror(gram_m)
    lower = jnp.linalg.cholesky(mass_gram)
    half = lower_solve(lower, stiff_gram)
    ritz_pencil = lower_solve(lower, jnp.transpose(half))
    return (search_dir, ritz_pencil)
```

```python
import functools

import jax
import jax.numpy as jnp
from jax import lax
from jax.experimental import pallas as pl
from jax.experimental.pallas import tpu as pltpu
from jax.sharding import PartitionSpec as P

JOINT_GAIN = 0.5
SPRING = (0.0, 0.1, 0.05, 0.025)
OFFSETS = [
    (step_z, step_y, step_x)
    for step_z in (-1, 0, 1)
    for step_y in (-1, 0, 1)
    for step_x in (-1, 0, 1)
    if (step_z, step_y, step_x) != (0, 0, 0)
]


def extended(shard, sides, width):
    for axis, dim in sides:
        peers, length = (lax.axis_size(axis), shard.shape[dim])
        up = [(i, (i + 1) % peers) for i in range(peers - 1)]
        down = [(j, i) for i, j in up]
        last = lax.slice_in_dim(shard, length - width, length, axis=dim)
        first = lax.slice_in_dim(shard, 0, width, axis=dim)
        before = lax.ppermute(last, axis, up)
        after = lax.ppermute(first, axis, down)
        shard = jnp.concatenate([before, shard, after], axis=dim)
    return shard


def lower_solve(lower, matrix):
    return lax.linalg.triangular_solve(lower, matrix, left_side=True, lower=True)


def edge_weights(kappa_pad):
    padded = jnp.pad(kappa_pad.astype(jnp.float32), ((0, 0), (1, 1), (1, 1)))
    depth = padded.shape[0] - 2
    height = padded.shape[1] - 2
    breadth = padded.shape[2] - 2
    centre = padded[1:-1, 1:-1, 1:-1]
    weights = []
    summed = jnp.zeros(centre.shape, jnp.float32)
    for offset in OFFSETS:
        step_z, step_y, step_x = offset
        other = padded[
            1 + step_z : 1 + step_z + depth,
            1 + step_y : 1 + step_y + height,
            1 + step_x : 1 + step_x + breadth,
        ]
        reach = abs(step_z) + abs(step_y) + abs(step_x)
        weight = SPRING[reach] * 2.0 * centre * other / (centre + other)
        weights.append(weight)
        summed = summed + weight
    return (weights, summed)


def apply_stencil(values_pad, weights, summed):
    padded = jnp.pad(values_pad, ((0, 0), (0, 0), (1, 1), (1, 1)))
    depth = padded.shape[1] - 2
    height = padded.shape[2] - 2
    breadth = padded.shape[3] - 2
    accum = jnp.zeros((padded.shape[0], depth, height, breadth), jnp.float32)
    for offset, weight in zip(OFFSETS, weights):
        step_z, step_y, step_x = offset
        other = padded[
            :,
            1 + step_z : 1 + step_z + depth,
            1 + step_y : 1 + step_y + height,
            1 + step_x : 1 + step_x + breadth,
        ]
        accum = accum + weight[None] * other.astype(jnp.float32)
    centre = padded[:, 1:-1, 1:-1, 1:-1].astype(jnp.float32)
    return summed[None] * centre - accum


def joint_apply(result, sent, recv, node_ids, joint_w):
    width = result.shape[0]
    delta = joint_w.reshape(1, -1) * (sent.astype(jnp.float32) - recv.astype(jnp.float32)).reshape(
        width, -1
    )
    return result.reshape(width, -1).at[:, node_ids].add(delta).reshape(result.shape)


def mirror(matrix):
    return jnp.triu(matrix) + jnp.transpose(jnp.triu(matrix, 1))


def fetch(block, node_ids, sections, capacity):
    padded = extended(block, (("bulk", 1),), 1)
    width = block.shape[0]
    sent = jnp.take(block.reshape(width, -1), node_ids, axis=1).reshape(width, sections, capacity)
    recv = lax.all_to_all(sent, "sec", split_axis=1, concat_axis=1, tiled=True)
    return (padded, sent, recv)


def total_kernel(
    ns, nb, src, out, acc, full, land_s, land_b, s1, r1, s2, r2, s3, r3, s4, r4
):
    me_s, me_b = lax.axis_index("sec"), lax.axis_index("bulk")

    def sec(k):
        return lax.rem(me_s + k, ns)

    def bulk(k):
        return lax.rem(me_b + k, nb)

    def push(source, target, send, recv, device):
        copy = pltpu.make_async_remote_copy(
            src_ref=source,
            dst_ref=target,
            send_sem=send,
            recv_sem=recv,
            device_id=device,
            device_id_type=pl.DeviceIdType.MESH,
        )
        copy.start()
        return copy

    barrier = pltpu.get_barrier_semaphore()
    for k in range(1, ns):
        pl.semaphore_signal(
            barrier, inc=1, device_id=(sec(k), me_b), device_id_type=pl.DeviceIdType.MESH
        )
    for k in range(1, nb):
        pl.semaphore_signal(
            barrier, inc=1, device_id=(me_s, bulk(k)), device_id_type=pl.DeviceIdType.MESH
        )
    pl.semaphore_wait(barrier, ns - 1 + nb - 1)

    copies = [
        push(src.at[sec(k)], land_s.at[k - 1], s1.at[k - 1], r1.at[k - 1], (sec(k), me_b))
        for k in range(1, ns)
    ]
    for copy in copies:
        copy.wait()
    value = src[me_s]
    for k in range(1, ns):
        value = value + land_s[k - 1]
    acc[...] = value

    copies = [
        push(acc.at[bulk(k)], land_b.at[k - 1], s2.at[k - 1], r2.at[k - 1], (me_s, bulk(k)))
        for k in range(1, nb)
    ]
    for copy in copies:
        copy.wait()
    value = acc[me_b]
    for k in range(1, nb):
        value = value + land_b[k - 1]
    full[me_s, me_b] = value

    copies = [
        push(
            full.at[me_s, me_b],
            full.at[me_s, me_b],
            s3.at[k - 1],
            r3.at[k - 1],
            (me_s, bulk(k)),
        )
        for k in range(1, nb)
    ]
    for copy in copies:
        copy.wait()
    copies = [
        push(full.at[me_s], full.at[me_s], s4.at[k - 1], r4.at[k - 1], (sec(k), me_b))
        for k in range(1, ns)
    ]
    for copy in copies:
        copy.wait()
    out[...] = full[...]


def total(parts):
    ns, nb, t = parts.shape[:3]
    rest = parts.shape[2:]
    dma = pltpu.SemaphoreType.DMA
    return pl.pallas_call(
        functools.partial(total_kernel, ns, nb),
        out_shape=jax.ShapeDtypeStruct(parts.shape, jnp.float32),
        in_specs=[pl.BlockSpec(memory_space=pltpu.VMEM)],
        out_specs=pl.BlockSpec(memory_space=pltpu.VMEM),
        scratch_shapes=[
            pltpu.VMEM((nb,) + rest, jnp.float32),
            pltpu.VMEM((ns, nb) + rest, jnp.float32),
            pltpu.VMEM((ns - 1, nb) + rest, jnp.float32),
            pltpu.VMEM((nb - 1,) + rest, jnp.float32),
            dma((ns - 1,)),
            dma((ns - 1,)),
            dma((nb - 1,)),
            dma((nb - 1,)),
            dma((nb - 1,)),
            dma((nb - 1,)),
            dma((ns - 1,)),
            dma((ns - 1,)),
        ],
        compiler_params=pltpu.CompilerParams(
            collective_id=0, has_side_effects=True, vmem_limit_bytes=32 * 2**20
        ),
    )(parts)


def whole_grams(gram_k, gram_mt):
    size = gram_k.shape[0]
    wide = -(-(size + 1) // 128) * 128
    rows = lax.broadcasted_iota(jnp.int32, (size, size), 0)
    cols = lax.broadcasted_iota(jnp.int32, (size, size), 1)
    packed = jnp.where(cols >= rows, gram_k, gram_mt)
    diag = jnp.sum(jnp.where(cols == rows, gram_mt, 0.0), axis=1, keepdims=True)
    extra = jnp.pad(diag, ((0, 0), (0, wide - size - 1)))
    packed = jnp.concatenate([packed, extra], axis=1)
    ns, nb = lax.axis_size("sec"), lax.axis_size("bulk")
    tiles = (size // 8) * (wide // 128)
    each = -(-tiles // (ns * nb))
    flat = packed.reshape(size // 8, 8, wide // 128, 128).transpose(0, 2, 1, 3)
    flat = flat.reshape(tiles, 8, 128)
    flat = jnp.pad(flat, ((0, ns * nb * each - tiles), (0, 0), (0, 0)))
    flat = total(flat.reshape(ns, nb, each, 8, 128)).reshape(ns * nb * each, 8, 128)
    flat = flat[:tiles].reshape(size // 8, wide // 128, 8, 128).transpose(0, 2, 1, 3)
    packed = flat.reshape(size, wide)
    square, diag = packed[:, :size], packed[:, size : size + 1]
    turned = square.T
    stiff_gram = jnp.where(cols >= rows, square, turned)
    mass_gram = jnp.where(cols < rows, square, jnp.where(cols == rows, diag, turned))
    return stiff_gram, mass_gram


def on_device(
    modes_x, modes_p, ritz_values, node_types, stiff_table, mass_table, joint_nodes, joint_count
):
    modes = modes_x.shape[0]
    sections = joint_nodes.shape[2]
    capacity = joint_nodes.shape[3]
    columns = 3 * modes
    levels = jnp.arange(stiff_table.shape[0], dtype=jnp.int32)[:, None, None, None]
    chosen = node_types[0][None] == levels
    kappa = jnp.sum(jnp.where(chosen, stiff_table[:, None, None, None], 0.0), axis=0).astype(
        jnp.bfloat16
    )
    mass = jnp.sum(jnp.where(chosen, mass_table[:, None, None, None], 0.0), axis=0)
    node_ids = joint_nodes[0, 0].reshape(-1)
    live = (jnp.arange(capacity, dtype=jnp.int32)[None, :] < joint_count[0, 0][:, None]).astype(
        jnp.float32
    )
    x_local = modes_x[:, 0]
    p_local = modes_p[:, 0]
    k_row = x_local.shape[0]
    first = jnp.concatenate([x_local, kappa[None]], axis=0)
    padded, sent, recv = fetch(first, node_ids, sections, capacity)
    weights, summed = edge_weights(padded[k_row])
    own = sent[k_row].astype(jnp.float32)
    other = recv[k_row].astype(jnp.float32)
    joint_w = JOINT_GAIN * 2.0 * own * other / (own + other) * live
    diag_full = summed.reshape(-1).at[node_ids].add(joint_w.reshape(-1)).reshape(summed.shape)
    stiff_first = joint_apply(
        apply_stencil(padded[:k_row], weights, summed),
        sent[:k_row],
        recv[:k_row],
        node_ids,
        joint_w,
    )
    resid = (
        stiff_first - mass[None] * x_local.astype(jnp.float32) * ritz_values[:, None, None, None]
    )
    search_local = (resid / diag_full[None]).astype(jnp.bfloat16)
    second = jnp.concatenate([search_local, p_local], axis=0)
    padded_two, sent_two, recv_two = fetch(second, node_ids, sections, capacity)
    stiff_wp = joint_apply(
        apply_stencil(padded_two, weights, summed), sent_two, recv_two, node_ids, joint_w
    )
    span = jnp.concatenate([x_local, second], axis=0).reshape(columns, -1)
    stiff_span = (
        jnp.concatenate([stiff_first, stiff_wp], axis=0).astype(jnp.bfloat16).reshape(columns, -1)
    )
    mass_span = (mass.reshape(1, -1) * span.astype(jnp.float32)).astype(jnp.bfloat16)
    contract = (((1,), (1,)), ((), ()))
    gram_k = lax.dot_general(span, stiff_span, contract, preferred_element_type=jnp.float32)
    gram_mt = lax.dot_general(mass_span, span, contract, preferred_element_type=jnp.float32)
    stiff_gram, mass_gram = whole_grams(gram_k, gram_mt)
    lower = jnp.linalg.cholesky(mass_gram)
    half = lower_solve(lower, stiff_gram)
    ritz_pencil = lower_solve(lower, jnp.transpose(half))
    return (search_local[:, None], ritz_pencil)


def solution(mesh):
    placed = (
        P(None, "sec", "bulk", None, None),
        P(None, "sec", "bulk", None, None),
        P(),
        P("sec", "bulk", None, None),
        P(),
        P(),
        P("sec", "bulk", None, None),
        P("sec", "bulk", None),
    )
    return jax.shard_map(
        on_device,
        mesh=mesh,
        in_specs=placed,
        out_specs=(P(None, "sec", "bulk", None, None), P()),
        check_vma=False,
    )
```

```python
import functools

import jax
import jax.numpy as jnp
from jax import lax
from jax.experimental import pallas as pl
from jax.experimental.pallas import tpu as pltpu
from jax.sharding import PartitionSpec as P

JOINT_GAIN = 0.5
PANEL = 32
GROUP = 4
SPRING = (0.0, 0.1, 0.05, 0.025)
OFFSETS = [
    (step_z, step_y, step_x)
    for step_z in (-1, 0, 1)
    for step_y in (-1, 0, 1)
    for step_x in (-1, 0, 1)
    if (step_z, step_y, step_x) != (0, 0, 0)
]


def extended(shard, sides, width):
    for axis, dim in sides:
        peers, length = (lax.axis_size(axis), shard.shape[dim])
        up = [(i, (i + 1) % peers) for i in range(peers - 1)]
        down = [(j, i) for i, j in up]
        last = lax.slice_in_dim(shard, length - width, length, axis=dim)
        first = lax.slice_in_dim(shard, 0, width, axis=dim)
        before = lax.ppermute(last, axis, up)
        after = lax.ppermute(first, axis, down)
        shard = jnp.concatenate([before, shard, after], axis=dim)
    return shard


def edge_weights(kappa_pad):
    padded = jnp.pad(kappa_pad.astype(jnp.float32), ((0, 0), (1, 1), (1, 1)))
    depth = padded.shape[0] - 2
    height = padded.shape[1] - 2
    breadth = padded.shape[2] - 2
    centre = padded[1:-1, 1:-1, 1:-1]
    weights = []
    summed = jnp.zeros(centre.shape, jnp.float32)
    for offset in OFFSETS:
        step_z, step_y, step_x = offset
        other = padded[
            1 + step_z : 1 + step_z + depth,
            1 + step_y : 1 + step_y + height,
            1 + step_x : 1 + step_x + breadth,
        ]
        reach = abs(step_z) + abs(step_y) + abs(step_x)
        weight = SPRING[reach] * 2.0 * centre * other / (centre + other)
        weights.append(weight)
        summed = summed + weight
    return (weights, summed)


def apply_stencil(values_pad, weights, summed):
    padded = jnp.pad(values_pad, ((0, 0), (0, 0), (1, 1), (1, 1)))
    depth = padded.shape[1] - 2
    height = padded.shape[2] - 2
    breadth = padded.shape[3] - 2
    accum = jnp.zeros((padded.shape[0], depth, height, breadth), jnp.float32)
    for offset, weight in zip(OFFSETS, weights):
        step_z, step_y, step_x = offset
        other = padded[
            :,
            1 + step_z : 1 + step_z + depth,
            1 + step_y : 1 + step_y + height,
            1 + step_x : 1 + step_x + breadth,
        ]
        accum = accum + weight[None] * other.astype(jnp.float32)
    centre = padded[:, 1:-1, 1:-1, 1:-1].astype(jnp.float32)
    return summed[None] * centre - accum


def joint_apply(result, sent, recv, node_ids, joint_w):
    width = result.shape[0]
    delta = joint_w.reshape(1, -1) * (sent.astype(jnp.float32) - recv.astype(jnp.float32)).reshape(
        width, -1
    )
    return result.reshape(width, -1).at[:, node_ids].add(delta).reshape(result.shape)


def mirror(matrix):
    return jnp.triu(matrix) + jnp.transpose(jnp.triu(matrix, 1))


def fetch(block, node_ids, sections, capacity):
    padded = extended(block, (("bulk", 1),), 1)
    width = block.shape[0]
    sent = jnp.take(block.reshape(width, -1), node_ids, axis=1).reshape(width, sections, capacity)
    recv = lax.all_to_all(sent, "sec", split_axis=1, concat_axis=1, tiled=True)
    return (padded, sent, recv)


def total_kernel(
    ns, nb, src, out, acc, full, land_s, land_b, s1, r1, s2, r2, s3, r3, s4, r4
):
    me_s, me_b = lax.axis_index("sec"), lax.axis_index("bulk")

    def sec(k):
        return lax.rem(me_s + k, ns)

    def bulk(k):
        return lax.rem(me_b + k, nb)

    def push(source, target, send, recv, device):
        copy = pltpu.make_async_remote_copy(
            src_ref=source,
            dst_ref=target,
            send_sem=send,
            recv_sem=recv,
            device_id=device,
            device_id_type=pl.DeviceIdType.MESH,
        )
        copy.start()
        return copy

    barrier = pltpu.get_barrier_semaphore()
    for k in range(1, ns):
        pl.semaphore_signal(
            barrier, inc=1, device_id=(sec(k), me_b), device_id_type=pl.DeviceIdType.MESH
        )
    for k in range(1, nb):
        pl.semaphore_signal(
            barrier, inc=1, device_id=(me_s, bulk(k)), device_id_type=pl.DeviceIdType.MESH
        )
    pl.semaphore_wait(barrier, ns - 1 + nb - 1)

    copies = [
        push(src.at[sec(k)], land_s.at[k - 1], s1.at[k - 1], r1.at[k - 1], (sec(k), me_b))
        for k in range(1, ns)
    ]
    for copy in copies:
        copy.wait()
    value = src[me_s]
    for k in range(1, ns):
        value = value + land_s[k - 1]
    acc[...] = value

    copies = [
        push(acc.at[bulk(k)], land_b.at[k - 1], s2.at[k - 1], r2.at[k - 1], (me_s, bulk(k)))
        for k in range(1, nb)
    ]
    for copy in copies:
        copy.wait()
    value = acc[me_b]
    for k in range(1, nb):
        value = value + land_b[k - 1]
    full[me_s, me_b] = value

    copies = [
        push(
            full.at[me_s, me_b],
            full.at[me_s, me_b],
            s3.at[k - 1],
            r3.at[k - 1],
            (me_s, bulk(k)),
        )
        for k in range(1, nb)
    ]
    for copy in copies:
        copy.wait()
    copies = [
        push(full.at[me_s], full.at[me_s], s4.at[k - 1], r4.at[k - 1], (sec(k), me_b))
        for k in range(1, ns)
    ]
    for copy in copies:
        copy.wait()
    out[...] = full[...]


def total(parts):
    ns, nb, t = parts.shape[:3]
    rest = parts.shape[2:]
    dma = pltpu.SemaphoreType.DMA
    return pl.pallas_call(
        functools.partial(total_kernel, ns, nb),
        out_shape=jax.ShapeDtypeStruct(parts.shape, jnp.float32),
        in_specs=[pl.BlockSpec(memory_space=pltpu.VMEM)],
        out_specs=pl.BlockSpec(memory_space=pltpu.VMEM),
        scratch_shapes=[
            pltpu.VMEM((nb,) + rest, jnp.float32),
            pltpu.VMEM((ns, nb) + rest, jnp.float32),
            pltpu.VMEM((ns - 1, nb) + rest, jnp.float32),
            pltpu.VMEM((nb - 1,) + rest, jnp.float32),
            dma((ns - 1,)),
            dma((ns - 1,)),
            dma((nb - 1,)),
            dma((nb - 1,)),
            dma((nb - 1,)),
            dma((nb - 1,)),
            dma((ns - 1,)),
            dma((ns - 1,)),
        ],
        compiler_params=pltpu.CompilerParams(
            collective_id=0, has_side_effects=True, vmem_limit_bytes=32 * 2**20
        ),
    )(parts)


def whole_grams(gram_k, gram_mt):
    size = gram_k.shape[0]
    wide = -(-(size + 1) // 128) * 128
    rows = lax.broadcasted_iota(jnp.int32, (size, size), 0)
    cols = lax.broadcasted_iota(jnp.int32, (size, size), 1)
    packed = jnp.where(cols >= rows, gram_k, gram_mt)
    diag = jnp.sum(jnp.where(cols == rows, gram_mt, 0.0), axis=1, keepdims=True)
    extra = jnp.pad(diag, ((0, 0), (0, wide - size - 1)))
    packed = jnp.concatenate([packed, extra], axis=1)
    ns, nb = lax.axis_size("sec"), lax.axis_size("bulk")
    tiles = (size // 8) * (wide // 128)
    each = -(-tiles // (ns * nb))
    flat = packed.reshape(size // 8, 8, wide // 128, 128).transpose(0, 2, 1, 3)
    flat = flat.reshape(tiles, 8, 128)
    flat = jnp.pad(flat, ((0, ns * nb * each - tiles), (0, 0), (0, 0)))
    flat = total(flat.reshape(ns, nb, each, 8, 128)).reshape(ns * nb * each, 8, 128)
    flat = flat[:tiles].reshape(size // 8, wide // 128, 8, 128).transpose(0, 2, 1, 3)
    packed = flat.reshape(size, wide)
    square, diag = packed[:, :size], packed[:, size : size + 1]
    turned = square.T
    stiff_gram = jnp.where(cols >= rows, square, turned)
    mass_gram = jnp.where(cols < rows, square, jnp.where(cols == rows, diag, turned))
    return stiff_gram, mass_gram


def diagonal_inverse(tile, off):
    row = lax.broadcasted_iota(jnp.int32, tile.shape, 0)
    lane = lax.broadcasted_iota(jnp.int32, tile.shape, 1)
    unit = (off + 64) % 128
    inside = jnp.logical_and(lane >= off, lane < off + PANEL)
    a = jnp.where(inside, tile, jnp.where(lane - unit == row, 1.0, 0.0))
    for k in range(0, PANEL, GROUP):
        cols = [jnp.broadcast_to(a[:, off + k + j : off + k + j + 1], a.shape) for j in range(GROUP)]
        heads = [a[k + j : k + j + 1, :] for j in range(GROUP)]
        for j in range(GROUP):
            pivot = cols[j][k + j : k + j + 1, :]
            scale = lax.rsqrt(pivot)
            scale = scale * (1.5 - 0.5 * pivot * scale * scale)
            heads[j] = heads[j] * scale
            cols[j] = cols[j] * jnp.broadcast_to(scale, a.shape)
            for i in range(j + 1, GROUP):
                low = cols[j][k + i : k + i + 1, :]
                heads[i] = heads[i] - low * heads[j]
                cols[i] = cols[i] - cols[j] * jnp.broadcast_to(low, a.shape)
        change = cols[0] * jnp.broadcast_to(heads[0], a.shape)
        for j in range(1, GROUP):
            change = change + cols[j] * jnp.broadcast_to(heads[j], a.shape)
        a = jnp.where(row >= k + GROUP, a - change, a)
        for j in range(GROUP):
            a = jnp.where(row == k + j, jnp.broadcast_to(heads[j], a.shape), a)
    a = pltpu.roll(a, (128 - unit) % 128, 1)
    return a[:, :PANEL]

def thirds(value):
    high = value.astype(jnp.bfloat16)
    rest = value - high.astype(jnp.float32)
    mid = rest.astype(jnp.bfloat16)
    low = (rest - mid.astype(jnp.float32)).astype(jnp.bfloat16)
    return high, mid, low

def pencil_kernel(size, wide, mass, stiff, out, work):
    row = lax.broadcasted_iota(jnp.int32, (wide, wide), 0)
    lane = lax.broadcasted_iota(jnp.int32, (wide, wide), 1)
    work[:, :wide] = mass[...]
    work[:, wide:] = jnp.where(row == lane, 1.0, 0.0)
    highest = lax.Precision.HIGHEST
    for p in range(0, size, PANEL):
        home = p // 128 * 128
        after = (p + PANEL) // 128 * 128
        stop = wide + home + 128
        inverse = diagonal_inverse(work[p : p + PANEL, home : home + 128], p - home)
        strip = jnp.dot(inverse, work[p : p + PANEL, home:stop], precision=highest, preferred_element_type=jnp.float32)
        work[p : p + PANEL, home:stop] = strip
        if p + PANEL < size:
            strip = strip[:, after - home :]
            high, mid, low = thirds(strip)
            left = jnp.concatenate([high, high, mid, mid, high, low], axis=0)[:, : wide - after]
            right = jnp.concatenate([high, mid, high, mid, low, high], axis=0)
            change = lax.dot_general(left, right, (((0,), (0,)), ((), ())), preferred_element_type=jnp.float32)
            which = after + lax.broadcasted_iota(jnp.int32, change.shape, 0)
            work[after:, after:stop] = work[after:, after:stop] - jnp.where(which >= p + PANEL, change, 0.0)
    inverse = jnp.where(lane <= row, work[:, wide:], 0.0)
    half = jnp.dot(inverse, stiff[...], precision=highest, preferred_element_type=jnp.float32)
    out[...] = lax.dot_general(half, inverse, (((1,), (1,)), ((), ())), precision=highest, preferred_element_type=jnp.float32)

def pencil(mass_gram, stiff_gram):
    size = mass_gram.shape[0]
    wide = -(-size // 128) * 128
    grown = ((0, wide - size), (0, wide - size))
    result = pl.pallas_call(
        functools.partial(pencil_kernel, size, wide),
        out_shape=jax.ShapeDtypeStruct((wide, wide), jnp.float32),
        scratch_shapes=[pltpu.VMEM((wide, 2 * wide), jnp.float32)],
        compiler_params=pltpu.CompilerParams(vmem_limit_bytes=32 * 2**20),
    )(jnp.pad(mass_gram, grown), jnp.pad(stiff_gram, grown))
    return result[:size, :size]


def on_device(
    modes_x, modes_p, ritz_values, node_types, stiff_table, mass_table, joint_nodes, joint_count
):
    modes = modes_x.shape[0]
    sections = joint_nodes.shape[2]
    capacity = joint_nodes.shape[3]
    columns = 3 * modes
    levels = jnp.arange(stiff_table.shape[0], dtype=jnp.int32)[:, None, None, None]
    chosen = node_types[0][None] == levels
    kappa = jnp.sum(jnp.where(chosen, stiff_table[:, None, None, None], 0.0), axis=0).astype(
        jnp.bfloat16
    )
    mass = jnp.sum(jnp.where(chosen, mass_table[:, None, None, None], 0.0), axis=0)
    node_ids = joint_nodes[0, 0].reshape(-1)
    live = (jnp.arange(capacity, dtype=jnp.int32)[None, :] < joint_count[0, 0][:, None]).astype(
        jnp.float32
    )
    x_local = modes_x[:, 0]
    p_local = modes_p[:, 0]
    k_row = x_local.shape[0]
    first = jnp.concatenate([x_local, kappa[None]], axis=0)
    padded, sent, recv = fetch(first, node_ids, sections, capacity)
    weights, summed = edge_weights(padded[k_row])
    own = sent[k_row].astype(jnp.float32)
    other = recv[k_row].astype(jnp.float32)
    joint_w = JOINT_GAIN * 2.0 * own * other / (own + other) * live
    diag_full = summed.reshape(-1).at[node_ids].add(joint_w.reshape(-1)).reshape(summed.shape)
    stiff_first = joint_apply(
        apply_stencil(padded[:k_row], weights, summed),
        sent[:k_row],
        recv[:k_row],
        node_ids,
        joint_w,
    )
    resid = (
        stiff_first - mass[None] * x_local.astype(jnp.float32) * ritz_values[:, None, None, None]
    )
    search_local = (resid / diag_full[None]).astype(jnp.bfloat16)
    second = jnp.concatenate([search_local, p_local], axis=0)
    padded_two, sent_two, recv_two = fetch(second, node_ids, sections, capacity)
    stiff_wp = joint_apply(
        apply_stencil(padded_two, weights, summed), sent_two, recv_two, node_ids, joint_w
    )
    span = jnp.concatenate([x_local, second], axis=0).reshape(columns, -1)
    stiff_span = (
        jnp.concatenate([stiff_first, stiff_wp], axis=0).astype(jnp.bfloat16).reshape(columns, -1)
    )
    mass_span = (mass.reshape(1, -1) * span.astype(jnp.float32)).astype(jnp.bfloat16)
    contract = (((1,), (1,)), ((), ()))
    gram_k = lax.dot_general(span, stiff_span, contract, preferred_element_type=jnp.float32)
    gram_mt = lax.dot_general(mass_span, span, contract, preferred_element_type=jnp.float32)
    stiff_gram, mass_gram = whole_grams(gram_k, gram_mt)
    ritz_pencil = pencil(mass_gram, stiff_gram)
    return (search_local[:, None], ritz_pencil)


def solution(mesh):
    placed = (
        P(None, "sec", "bulk", None, None),
        P(None, "sec", "bulk", None, None),
        P(),
        P("sec", "bulk", None, None),
        P(),
        P(),
        P("sec", "bulk", None, None),
        P("sec", "bulk", None),
    )
    return jax.shard_map(
        on_device,
        mesh=mesh,
        in_specs=placed,
        out_specs=(P(None, "sec", "bulk", None, None), P()),
        check_vma=False,
    )
```

```python
import functools

import jax
import jax.numpy as jnp
from jax import lax
from jax.experimental import pallas as pl
from jax.experimental.pallas import tpu as pltpu
from jax.sharding import PartitionSpec as P

JOINT_GAIN = 0.5
PANEL = 32
GROUP = 4
SPRING = (0.0, 0.1, 0.05, 0.025)
OFFSETS = [
    (step_z, step_y, step_x)
    for step_z in (-1, 0, 1)
    for step_y in (-1, 0, 1)
    for step_x in (-1, 0, 1)
    if (step_z, step_y, step_x) != (0, 0, 0)
]


def edge_weights(kappa_pad):
    padded = jnp.pad(kappa_pad.astype(jnp.float32), ((0, 0), (1, 1), (1, 1)))
    depth = padded.shape[0] - 2
    height = padded.shape[1] - 2
    breadth = padded.shape[2] - 2
    centre = padded[1:-1, 1:-1, 1:-1]
    weights = []
    summed = jnp.zeros(centre.shape, jnp.float32)
    for offset in OFFSETS:
        step_z, step_y, step_x = offset
        other = padded[
            1 + step_z : 1 + step_z + depth,
            1 + step_y : 1 + step_y + height,
            1 + step_x : 1 + step_x + breadth,
        ]
        reach = abs(step_z) + abs(step_y) + abs(step_x)
        weight = SPRING[reach] * 2.0 * centre * other / (centre + other)
        weights.append(weight)
        summed = summed + weight
    return (weights, summed)


def total_kernel(
    ns, nb, src, out, acc, full, land_s, land_b, s1, r1, s2, r2, s3, r3, s4, r4
):
    me_s, me_b = lax.axis_index("sec"), lax.axis_index("bulk")

    def sec(k):
        return lax.rem(me_s + k, ns)

    def bulk(k):
        return lax.rem(me_b + k, nb)

    def push(source, target, send, recv, device):
        copy = pltpu.make_async_remote_copy(
            src_ref=source,
            dst_ref=target,
            send_sem=send,
            recv_sem=recv,
            device_id=device,
            device_id_type=pl.DeviceIdType.MESH,
        )
        copy.start()
        return copy

    barrier = pltpu.get_barrier_semaphore()
    for k in range(1, ns):
        pl.semaphore_signal(
            barrier, inc=1, device_id=(sec(k), me_b), device_id_type=pl.DeviceIdType.MESH
        )
    for k in range(1, nb):
        pl.semaphore_signal(
            barrier, inc=1, device_id=(me_s, bulk(k)), device_id_type=pl.DeviceIdType.MESH
        )
    pl.semaphore_wait(barrier, ns - 1 + nb - 1)

    copies = [
        push(src.at[sec(k)], land_s.at[k - 1], s1.at[k - 1], r1.at[k - 1], (sec(k), me_b))
        for k in range(1, ns)
    ]
    for copy in copies:
        copy.wait()
    value = src[me_s]
    for k in range(1, ns):
        value = value + land_s[k - 1]
    acc[...] = value

    copies = [
        push(acc.at[bulk(k)], land_b.at[k - 1], s2.at[k - 1], r2.at[k - 1], (me_s, bulk(k)))
        for k in range(1, nb)
    ]
    for copy in copies:
        copy.wait()
    value = acc[me_b]
    for k in range(1, nb):
        value = value + land_b[k - 1]
    full[me_s, me_b] = value

    copies = [
        push(
            full.at[me_s, me_b],
            full.at[me_s, me_b],
            s3.at[k - 1],
            r3.at[k - 1],
            (me_s, bulk(k)),
        )
        for k in range(1, nb)
    ]
    for copy in copies:
        copy.wait()
    copies = [
        push(full.at[me_s], full.at[me_s], s4.at[k - 1], r4.at[k - 1], (sec(k), me_b))
        for k in range(1, ns)
    ]
    for copy in copies:
        copy.wait()
    out[...] = full[...]


def total(parts):
    ns, nb, t = parts.shape[:3]
    rest = parts.shape[2:]
    dma = pltpu.SemaphoreType.DMA
    return pl.pallas_call(
        functools.partial(total_kernel, ns, nb),
        out_shape=jax.ShapeDtypeStruct(parts.shape, jnp.float32),
        in_specs=[pl.BlockSpec(memory_space=pltpu.VMEM)],
        out_specs=pl.BlockSpec(memory_space=pltpu.VMEM),
        scratch_shapes=[
            pltpu.VMEM((nb,) + rest, jnp.float32),
            pltpu.VMEM((ns, nb) + rest, jnp.float32),
            pltpu.VMEM((ns - 1, nb) + rest, jnp.float32),
            pltpu.VMEM((nb - 1,) + rest, jnp.float32),
            dma((ns - 1,)),
            dma((ns - 1,)),
            dma((nb - 1,)),
            dma((nb - 1,)),
            dma((nb - 1,)),
            dma((nb - 1,)),
            dma((ns - 1,)),
            dma((ns - 1,)),
        ],
        compiler_params=pltpu.CompilerParams(
            collective_id=0, has_side_effects=True, vmem_limit_bytes=32 * 2**20
        ),
    )(parts)


def whole_grams(gram_k, gram_mt):
    size = gram_k.shape[0]
    wide = -(-(size + 1) // 128) * 128
    rows = lax.broadcasted_iota(jnp.int32, (size, size), 0)
    cols = lax.broadcasted_iota(jnp.int32, (size, size), 1)
    packed = jnp.where(cols >= rows, gram_k, gram_mt)
    diag = jnp.sum(jnp.where(cols == rows, gram_mt, 0.0), axis=1, keepdims=True)
    extra = jnp.pad(diag, ((0, 0), (0, wide - size - 1)))
    packed = jnp.concatenate([packed, extra], axis=1)
    ns, nb = lax.axis_size("sec"), lax.axis_size("bulk")
    tiles = (size // 8) * (wide // 128)
    each = -(-tiles // (ns * nb))
    flat = packed.reshape(size // 8, 8, wide // 128, 128).transpose(0, 2, 1, 3)
    flat = flat.reshape(tiles, 8, 128)
    flat = jnp.pad(flat, ((0, ns * nb * each - tiles), (0, 0), (0, 0)))
    flat = total(flat.reshape(ns, nb, each, 8, 128)).reshape(ns * nb * each, 8, 128)
    flat = flat[:tiles].reshape(size // 8, wide // 128, 8, 128).transpose(0, 2, 1, 3)
    packed = flat.reshape(size, wide)
    square, diag = packed[:, :size], packed[:, size : size + 1]
    turned = square.T
    stiff_gram = jnp.where(cols >= rows, square, turned)
    mass_gram = jnp.where(cols < rows, square, jnp.where(cols == rows, diag, turned))
    return stiff_gram, mass_gram


def diagonal_inverse(tile, off):
    row = lax.broadcasted_iota(jnp.int32, tile.shape, 0)
    lane = lax.broadcasted_iota(jnp.int32, tile.shape, 1)
    unit = (off + 64) % 128
    inside = jnp.logical_and(lane >= off, lane < off + PANEL)
    a = jnp.where(inside, tile, jnp.where(lane - unit == row, 1.0, 0.0))
    for k in range(0, PANEL, GROUP):
        cols = [jnp.broadcast_to(a[:, off + k + j : off + k + j + 1], a.shape) for j in range(GROUP)]
        heads = [a[k + j : k + j + 1, :] for j in range(GROUP)]
        for j in range(GROUP):
            pivot = cols[j][k + j : k + j + 1, :]
            scale = lax.rsqrt(pivot)
            scale = scale * (1.5 - 0.5 * pivot * scale * scale)
            heads[j] = heads[j] * scale
            cols[j] = cols[j] * jnp.broadcast_to(scale, a.shape)
            for i in range(j + 1, GROUP):
                low = cols[j][k + i : k + i + 1, :]
                heads[i] = heads[i] - low * heads[j]
                cols[i] = cols[i] - cols[j] * jnp.broadcast_to(low, a.shape)
        change = cols[0] * jnp.broadcast_to(heads[0], a.shape)
        for j in range(1, GROUP):
            change = change + cols[j] * jnp.broadcast_to(heads[j], a.shape)
        a = jnp.where(row >= k + GROUP, a - change, a)
        for j in range(GROUP):
            a = jnp.where(row == k + j, jnp.broadcast_to(heads[j], a.shape), a)
    a = pltpu.roll(a, (128 - unit) % 128, 1)
    return a[:, :PANEL]

def thirds(value):
    high = value.astype(jnp.bfloat16)
    rest = value - high.astype(jnp.float32)
    mid = rest.astype(jnp.bfloat16)
    low = (rest - mid.astype(jnp.float32)).astype(jnp.bfloat16)
    return high, mid, low

def pencil_kernel(size, wide, mass, stiff, out, work):
    row = lax.broadcasted_iota(jnp.int32, (wide, wide), 0)
    lane = lax.broadcasted_iota(jnp.int32, (wide, wide), 1)
    work[:, :wide] = mass[...]
    work[:, wide:] = jnp.where(row == lane, 1.0, 0.0)
    highest = lax.Precision.HIGHEST
    for p in range(0, size, PANEL):
        home = p // 128 * 128
        after = (p + PANEL) // 128 * 128
        stop = wide + home + 128
        inverse = diagonal_inverse(work[p : p + PANEL, home : home + 128], p - home)
        strip = jnp.dot(inverse, work[p : p + PANEL, home:stop], precision=highest, preferred_element_type=jnp.float32)
        work[p : p + PANEL, home:stop] = strip
        if p + PANEL < size:
            strip = strip[:, after - home :]
            high, mid, low = thirds(strip)
            left = jnp.concatenate([high, high, mid, mid, high, low], axis=0)[:, : wide - after]
            right = jnp.concatenate([high, mid, high, mid, low, high], axis=0)
            change = lax.dot_general(left, right, (((0,), (0,)), ((), ())), preferred_element_type=jnp.float32)
            which = after + lax.broadcasted_iota(jnp.int32, change.shape, 0)
            work[after:, after:stop] = work[after:, after:stop] - jnp.where(which >= p + PANEL, change, 0.0)
    inverse = jnp.where(lane <= row, work[:, wide:], 0.0)
    half = jnp.dot(inverse, stiff[...], precision=highest, preferred_element_type=jnp.float32)
    out[...] = lax.dot_general(half, inverse, (((1,), (1,)), ((), ())), precision=highest, preferred_element_type=jnp.float32)

def pencil(mass_gram, stiff_gram):
    size = mass_gram.shape[0]
    wide = -(-size // 128) * 128
    grown = ((0, wide - size), (0, wide - size))
    result = pl.pallas_call(
        functools.partial(pencil_kernel, size, wide),
        out_shape=jax.ShapeDtypeStruct((wide, wide), jnp.float32),
        scratch_shapes=[pltpu.VMEM((wide, 2 * wide), jnp.float32)],
        compiler_params=pltpu.CompilerParams(vmem_limit_bytes=32 * 2**20),
    )(jnp.pad(mass_gram, grown), jnp.pad(stiff_gram, grown))
    return result[:size, :size]


def stencil_kernel(
    lines, depth, block, before, after, weights, joint, mass, diag, ritz, stiff, search, rows
):
    columns = block.shape[0]
    width = weights.shape[2]
    count = lines * depth
    zero = jnp.zeros((columns, width), jnp.float32)
    rows[0] = zero
    rows[count + 2 * lines + 1] = zero
    for i in range(lines):
        part = slice(i * width, (i + 1) * width)
        rows[1 + i] = before[:, part].astype(jnp.float32)
        rows[1 + lines + count + i] = after[:, part].astype(jnp.float32)
    for i in range(count):
        rows[1 + lines + i] = block[:, i * width : (i + 1) * width].astype(jnp.float32)

    def row(r, carry):
        place = pl.ds(pl.multiple_of(r * width, width), width)
        here = pl.ds(r, 1)
        for c in range(0, columns, 16):
            tile = slice(c, c + 16)
            sums = []
            for dx in range(3):
                value = None
                for near in range(9):
                    step = (near // 3 - 1) * lines + near % 3 - 1
                    term = weights[3 * near + dx, here, :] * rows[r + lines + 1 + step, tile, :]
                    value = term if value is None else value + term
                sums.append(value)
            value = sums[1] + pltpu.roll(sums[0], 1, 1) + pltpu.roll(sums[2], width - 1, 1)
            value = value + joint[tile, place]
            stiff[tile, place] = value.astype(jnp.bfloat16)
            if search is not None:
                centre = rows[r + lines + 1, tile, :]
                resid = value - mass[here, :] * centre * ritz[tile, :]
                search[tile, place] = (resid / diag[here, :]).astype(jnp.bfloat16)
        return carry

    lax.fori_loop(0, count, row, 0)


def stencil(block, before, after, weights, joint, depth, extra=None):
    columns, nodes = block.shape
    lines = weights.shape[1] // depth
    width = weights.shape[2]
    flat = jax.ShapeDtypeStruct((columns, nodes), jnp.bfloat16)
    vmem = pl.BlockSpec(memory_space=pltpu.VMEM)
    operands = [block, before, after, weights, joint]
    if extra is None:

        def body(a, b, c, d, e, stiff, rows):
            stencil_kernel(lines, depth, a, b, c, d, e, None, None, None, stiff, None, rows)

        outs = [flat]
    else:
        operands += list(extra)
        body = functools.partial(stencil_kernel, lines, depth)
        outs = [flat, flat]
    return pl.pallas_call(
        body,
        out_shape=outs,
        in_specs=[vmem] * len(operands),
        out_specs=[vmem] * len(outs),
        scratch_shapes=[
            pltpu.VMEM((lines * (depth + 2) + 2, columns, width), jnp.float32)
        ],
        compiler_params=pltpu.CompilerParams(vmem_limit_bytes=40 * 2**20),
        cost_estimate=pl.CostEstimate(
            flops=54 * columns * nodes, bytes_accessed=8 * columns * nodes, transcendentals=0
        ),
    )(*operands)


def swap(block, hot, layer):
    slabs, sections = lax.axis_size("bulk"), lax.axis_size("sec")
    up = [(i, i + 1) for i in range(slabs - 1)]
    down = [(i + 1, i) for i in range(slabs - 1)]
    contract = (((1,), (1,)), ((), ()))
    sent = lax.dot_general(block, hot, contract, preferred_element_type=jnp.float32)
    sent = sent.astype(jnp.bfloat16)
    capacity = hot.shape[0] // (sections - 1)
    got = []
    for k in range(1, sections):
        there = sections - k
        chunk = sent[:, (there - 1) * capacity : there * capacity]
        ring = [(i, (i + there) % sections) for i in range(sections)]
        got.append(lax.ppermute(chunk, "sec", ring))
    before = lax.ppermute(block[:, -layer:], "bulk", up)
    after = lax.ppermute(block[:, :layer], "bulk", down)
    return before, after, sent, jnp.concatenate(got, axis=1)


def scatter(values, hot):
    count = values.shape[0]
    high = lax.reduce_precision(values, 8, 7)
    mid = lax.reduce_precision(values - high, 8, 7)
    low = values - high - mid
    pieces = jnp.concatenate([high, mid, low], axis=0).astype(jnp.bfloat16)
    placed = jnp.dot(pieces, hot, preferred_element_type=jnp.float32)
    return placed[:count] + placed[count : 2 * count] + placed[2 * count :]


def on_device(
    modes_x, modes_p, ritz_values, node_types, stiff_table, mass_table, joint_nodes, joint_count
):
    modes = modes_x.shape[0]
    depth, lines, width = node_types.shape[1:]
    nodes = depth * lines * width
    layer = lines * width
    sections = joint_nodes.shape[2]
    capacity = joint_nodes.shape[3]
    columns = 3 * modes
    levels = jnp.arange(stiff_table.shape[0], dtype=jnp.int32)[:, None, None, None]
    chosen = node_types[0][None] == levels
    kappa = jnp.sum(jnp.where(chosen, stiff_table[:, None, None, None], 0.0), axis=0).astype(
        jnp.bfloat16
    )
    mass = jnp.sum(jnp.where(chosen, mass_table[:, None, None, None], 0.0), axis=0)

    order = lax.rem(lax.axis_index("sec") + jnp.arange(1, sections), sections)
    node_ids = jnp.take(joint_nodes[0, 0], order, axis=0).reshape(-1)
    counts = jnp.take(joint_count[0, 0], order)
    live = (jnp.arange(capacity, dtype=jnp.int32)[None, :] < counts[:, None]).reshape(-1)
    hot = (node_ids[:, None] == jnp.arange(nodes, dtype=jnp.int32)[None, :]).astype(jnp.bfloat16)

    x_local = modes_x.reshape(modes, nodes)
    p_local = modes_p.reshape(modes, nodes)
    fill = jnp.broadcast_to(kappa.reshape(1, nodes), (16, nodes))
    first = jnp.concatenate([x_local, p_local, fill], axis=0)
    before, after, sent, got = swap(first, hot, layer)
    k_row = 2 * modes

    kappa_pad = jnp.concatenate(
        [
            before[k_row].reshape(1, lines, width),
            kappa,
            after[k_row].reshape(1, lines, width),
        ],
        axis=0,
    )
    weights, summed = edge_weights(kappa_pad)
    stack = [-jnp.roll(w, offset[2], axis=2) for offset, w in zip(OFFSETS, weights)]
    stack.insert(13, summed)
    stack = jnp.stack(stack).reshape(27, depth * lines, width)

    own = sent[k_row].astype(jnp.float32)
    other = got[k_row].astype(jnp.float32)
    joint_w = JOINT_GAIN * 2.0 * own * other / (own + other) * live.astype(jnp.float32)
    delta = joint_w[None] * (sent.astype(jnp.float32) - got.astype(jnp.float32))
    delta = jnp.concatenate(
        [delta[:k_row], jnp.broadcast_to(joint_w[None], (16, joint_w.shape[0]))], axis=0
    )
    joint = scatter(delta, hot)
    diag = summed.reshape(depth * lines, width) + joint[k_row].reshape(depth * lines, width)
    ritz = jnp.broadcast_to(ritz_values[:, None], (modes, width))
    mass_rows = mass.reshape(depth * lines, width)
    stiff_x, search = stencil(
        x_local,
        before[:modes],
        after[:modes],
        stack,
        joint[:modes],
        depth,
        (mass_rows, diag, ritz),
    )
    before_w, after_w, sent_w, got_w = swap(search, hot, layer)
    stiff_p = stencil(
        p_local, before[modes:k_row], after[modes:k_row], stack, joint[modes:k_row], depth
    )[0]
    delta_w = joint_w[None] * (sent_w.astype(jnp.float32) - got_w.astype(jnp.float32))
    stiff_w = stencil(search, before_w, after_w, stack, scatter(delta_w, hot), depth)[0]

    span = jnp.concatenate([x_local, search, p_local], axis=0)
    stiff_span = jnp.concatenate([stiff_x, stiff_w, stiff_p], axis=0)
    mass_span = (mass.reshape(1, -1) * span.astype(jnp.float32)).astype(jnp.bfloat16)
    contract = (((1,), (1,)), ((), ()))
    gram_k = lax.dot_general(span, stiff_span, contract, preferred_element_type=jnp.float32)
    gram_mt = lax.dot_general(mass_span, span, contract, preferred_element_type=jnp.float32)
    stiff_gram, mass_gram = whole_grams(gram_k, gram_mt)
    ritz_pencil = pencil(mass_gram, stiff_gram)
    return (search.reshape(modes_x.shape), ritz_pencil)


def solution(mesh):
    placed = (
        P(None, "sec", "bulk", None, None),
        P(None, "sec", "bulk", None, None),
        P(),
        P("sec", "bulk", None, None),
        P(),
        P(),
        P("sec", "bulk", None, None),
        P("sec", "bulk", None),
    )
    return jax.shard_map(
        on_device,
        mesh=mesh,
        in_specs=placed,
        out_specs=(P(None, "sec", "bulk", None, None), P()),
        check_vma=False,
    )
```
